32 devices in a mesh: req: 8 (over z, y), tp: 4 (over x, core).
Axes of the slice: x: 2, y: 2, z: 4, core: 2. Of those that a mesh axis runs over, the one named last changes fastest.
Arguments:
- queries: bfloat16 [2048, 2048], P('req', 'tp'), may hold values from -160 to 160
- key_rows: bfloat16 [2048, 2048], P('req', 'tp'), may hold values from -6 to 6
- value_rows: bfloat16 [2048, 2048], P('req', 'tp'), may hold values from -6 to 6
- lengths: int32 [8, 4], P('req'), may hold values from 1 to 128, 256 in all within a row
- adapter_ids: int32 [8, 4], P('req'), may hold values from 0 to 7, as said below
- adapter_home: int32 [8], replicated, may hold values from 0 to 7, each once
- adapter_down: bfloat16 [8, 2048, 16], P('req', 'tp'), may hold values from -0.125 to 0.125
- adapter_up: bfloat16 [8, 16, 2048], P('req'), may hold values from -4 to 4
- output_weight: bfloat16 [2048, 2048], P('tp'), may hold values from -0.125 to 0.125
Outputs:
- block_output: bfloat16 [2048, 2048], P('req', 'tp')
The draws below stay inside these ranges and needn't reach their ends.
Inputs may be any that keep to these rules, and one draw needn't show every extreme that they name: `adapter_ids`: all prompts together name exactly 2 distinct adapters.
All inputs are finite; a program needn't handle non-finite values.
Results may differ from the reference program's by a relative error of at most 0.0055.
Values may be sent and summed in bfloat16 or wider, within the bound.
No kernel may reach another device: no remote copies, remote signals or barrier semaphores. Data moves between devices by JAX's collectives and lax.ppermute only.
A program may use at most 64 MiB of HBM per device.

```python
import math
import jax
import jax.numpy as jnp
import numpy as np
from jax import lax

D = 2048
HD = 128
RANK = 16
TOK_DEV = 256
SEQ_DEV = 4
AW = 2048
TOKENS = 2048
ADAPTERS = 8
USED = 2
N_REQ = 8


def shared_keys(key):
    return jax.random.truncated_normal(jax.random.fold_in(key, 7), -5.0, 5.0, (TOKENS, AW), jnp.float32)


def draw_key_rows(key, part):
    key_basis = shared_keys(key)
    return key_basis.astype(jnp.bfloat16)


def draw_queries(key, part):
    drawn_rows = jax.random.truncated_normal(jax.random.fold_in(key, 11), -5.0, 5.0, (TOKENS, AW), jnp.float32)
    return drawn_rows.astype(jnp.bfloat16)


def draw_adapter_ids(key, part):
    middle = jax.random.permutation(jax.random.fold_in(key, 1), ADAPTERS - 2)[:USED - 2] + 1
    picked = jnp.concatenate([jnp.array([0, ADAPTERS - 1], dtype=jnp.int32), middle.astype(jnp.int32)])
    spread = jax.random.permutation(jax.random.fold_in(key, 2), N_REQ * SEQ_DEV) % USED
    return picked[spread].reshape(N_REQ, SEQ_DEV).astype(jnp.int32)


def level_of(stream_key, dims, split, smallest, largest):
    def one(axis_at, shards_of):
        draws = jax.random.uniform(jax.random.fold_in(jax.random.fold_in(stream_key, 6), axis_at), (shards_of,), jnp.float32, smallest / len(split), largest / len(split))
        return jnp.repeat(jnp.exp(draws), dims[axis_at] // shards_of).reshape((-1,) + (1,) * (len(dims) - axis_at - 1))

    level = one(*split[0])
    for cut in split[1:]:
        level = level * one(*cut)
    return level


def profile(number_of, total, limit, lean):
    weights = [(1 << 20) // math.isqrt(rank ** lean) + 1 for rank in range(2, number_of + 1)]
    surplus, counts = total - limit - (number_of - 1), [1] * (number_of - 1)
    while surplus > 0:
        candidates = [i for i in range(number_of - 1) if counts[i] < limit]
        pool, remaining = sum([weights[i] for i in candidates]), surplus
        for i in candidates:
            more = min(limit - counts[i], max(1, remaining * weights[i] // pool), surplus)
            counts[i] = counts[i] + more
            surplus = surplus - more
    return np.array([limit] + counts)


def ragged(stream_key, number_of, total, bound, lean):
    if number_of == 2:
        one = jax.random.randint(stream_key, (), max(1, total - bound), min(bound, total - 1) + 1)
        return jnp.stack([one, total - one])
    sizes = jnp.asarray(profile(number_of, total, bound, lean), jnp.int32)
    pairs = (number_of - 1) // 2
    giver, sink = sizes[1:1 + 2 * pairs:2], sizes[2:2 + 2 * pairs:2]
    room = jnp.minimum(giver - 1, bound - sink)
    passed = jax.random.randint(jax.random.fold_in(stream_key, 1), (pairs,), 0, 1 << 20) % (room + 1)
    sizes = sizes.at[1:1 + 2 * pairs:2].set(giver - passed).at[2:2 + 2 * pairs:2].set(sink + passed)
    return sizes[jax.random.permutation(jax.random.fold_in(stream_key, 2), number_of)]


def noise(own_key, shape, scale, reach, cuts=(), held_as=jnp.bfloat16):
    loudness = level_of(own_key, shape, cuts, -0.22, 0.18) if cuts else 1.0
    result = jax.random.normal(own_key, shape, jnp.float32) * scale * loudness
    return jnp.minimum(jnp.maximum(result, -reach), reach).astype(held_as)


def setup_inputs(seed: int = 0) -> dict:
    seeds = jax.random.split(jax.random.key(seed), 10)
    return {
        "queries": draw_queries(jax.random.fold_in(seeds[9], 71), 0),
        "key_rows": draw_key_rows(jax.random.fold_in(seeds[9], 71), 0),
        "value_rows": noise(seeds[2], (TOKENS, AW), 1.0, 6.0, ((0, 8), (1, 4))),
        "lengths": jax.vmap(lambda own: ragged(own, SEQ_DEV, TOK_DEV, TOK_DEV // 2, 2))(jax.random.split(seeds[3], N_REQ)).reshape((N_REQ, SEQ_DEV)).astype(jnp.int32),
        "adapter_ids": draw_adapter_ids(jax.random.fold_in(seeds[9], 71), 0),
        "adapter_home": jax.random.permutation(seeds[5], ADAPTERS).astype(jnp.int32),
        "adapter_down": noise(seeds[6], (ADAPTERS, AW, RANK), AW ** -0.5, 0.125, ((0, 8), (1, 4))),
        "adapter_up": noise(seeds[7], (ADAPTERS, RANK, D), 0.25, 4.0, ((0, 8),)),
        "output_weight": noise(seeds[8], (AW, D), AW ** -0.5, 0.125, ((0, 4),)),
    }


def segment_rows(length_row, row_total):
    boundary = jnp.cumsum(length_row)
    position = jnp.arange(row_total, dtype=jnp.int32)
    return lax.optimization_barrier(jnp.sum((position[:, None] >= boundary[None, :]).astype(jnp.int32), axis=1))

def attend(queries, key_rows, value_rows, segment):
    row_total = queries.shape[0]
    head_count = queries.shape[1] // HD
    shaped_q = queries.reshape(row_total, head_count, HD).astype(jnp.float32)
    shaped_k = key_rows.reshape(row_total, head_count, HD).astype(jnp.float32)
    shaped_v = value_rows.reshape(row_total, head_count, HD).astype(jnp.float32)
    scores = jnp.einsum('qhd,khd->hqk', shaped_q, shaped_k, precision=lax.Precision.HIGHEST) * (1.0 / math.sqrt(HD))
    position = jnp.arange(row_total, dtype=jnp.int32)
    allowed = (segment[:, None] == segment[None, :]) & (position[None, :] <= position[:, None])
    masked = jnp.where(allowed[None], scores, -1e+30)
    highest = lax.optimization_barrier(jnp.max(masked, axis=2, keepdims=True))
    exponent = jnp.where(allowed[None], jnp.exp(masked - highest), 0.0)
    weights = (exponent / lax.optimization_barrier(jnp.sum(exponent, axis=2, keepdims=True))).astype(jnp.bfloat16)
    mixed = jnp.einsum('hqk,khd->qhd', weights.astype(jnp.float32), shaped_v, precision=lax.Precision.HIGHEST)
    return mixed.reshape(row_total, head_count * HD).astype(jnp.bfloat16)

def lowrank_delta(rank_rows, onehot, factor_up):
    row_total, prompts = onehot.shape
    rank_size = rank_rows.shape[1]
    spread = (onehot[:, :, None] * rank_rows[:, None, :]).reshape(row_total, prompts * rank_size)
    upper = factor_up.astype(jnp.float32).reshape(prompts * rank_size, factor_up.shape[2])
    return jnp.dot(spread, upper, precision=lax.Precision.HIGHEST)

def reference(queries, key_rows, value_rows, lengths, adapter_ids, adapter_home, adapter_down, adapter_up, output_weight):
    groups = lengths.shape[0]
    width_all = queries.shape[1]
    grouped_q = queries.reshape(groups, TOK_DEV, width_all)
    grouped_k = key_rows.reshape(groups, TOK_DEV, width_all)
    grouped_v = value_rows.reshape(groups, TOK_DEV, width_all)

    def one_group(items):
        group_q, group_k, group_v, length_row, id_row = items
        segment = segment_rows(length_row, TOK_DEV)
        attended = attend(group_q, group_k, group_v, segment)
        base_rows = jnp.dot(attended, output_weight, preferred_element_type=jnp.float32)
        slot_rows = adapter_home[id_row]
        downs = adapter_down[slot_rows]
        uppers = adapter_up[slot_rows]
        per_prompt = jnp.einsum('ta,sar->str', attended.astype(jnp.float32), downs.astype(jnp.float32), precision=lax.Precision.HIGHEST)
        onehot = (segment[:, None] == jnp.arange(SEQ_DEV, dtype=jnp.int32)[None, :]).astype(jnp.float32)
        low_rank = jnp.einsum('ts,str->tr', onehot, per_prompt, precision=lax.Precision.HIGHEST)
        return (base_rows + lowrank_delta(low_rank, onehot, uppers)).astype(jnp.bfloat16)
    outputs = lax.map(one_group, (grouped_q, grouped_k, grouped_v, lengths, adapter_ids))
    return outputs.reshape(groups * TOK_DEV, outputs.shape[2])
```

```python
import functools
import math

import jax
import jax.numpy as jnp
from jax import lax
from jax.experimental import pallas as pl
from jax.experimental.pallas import tpu as pltpu
from jax.sharding import PartitionSpec as P

HD = 128
VMEM = pl.BlockSpec(memory_space=pltpu.VMEM)
SMEM = pl.BlockSpec(memory_space=pltpu.SMEM)
HBM = pl.BlockSpec(memory_space=pl.ANY)
F32, BF16 = jnp.float32, jnp.bfloat16


def dot(a, b, contract):
    return lax.dot_general(a, b, ((contract[0:1], contract[1:2]), ((), ())), preferred_element_type=F32)


def segment_start(len_ref, position):
    start, boundary = jnp.zeros_like(position), 0
    for s in range(len_ref.shape[1] - 1):
        boundary += len_ref[0, s]
        start = jnp.where(position >= boundary, boundary, start)
    return start


def prompt_mask(len_ref, s, position):
    low = sum((len_ref[0, i] for i in range(s)), jnp.int32(0))
    high = low + len_ref[0, s]
    return (position >= low) & (position < high)


def attend(q, k, v, len_ref, row0):
    rows, keys = q.shape[0], k.shape[0]
    scores = dot(q, k, (1, 1)) * (1.0 / math.sqrt(HD))
    query_at = row0 + lax.broadcasted_iota(jnp.int32, (rows, 1), 0)
    start = segment_start(len_ref, query_at)
    key_at = lax.broadcasted_iota(jnp.int32, (rows, keys), 1)
    masked = jnp.where((key_at >= start) & (key_at <= query_at), scores, -1e30)
    exponent = jnp.exp(masked - jnp.max(masked, axis=1, keepdims=True))
    weights = exponent * (1.0 / jnp.sum(exponent, axis=1, keepdims=True))
    return dot(weights.astype(BF16), v, (1, 0)).astype(BF16)


def attend_kernel(col_far, col_mid, len_ref, q_ref, k_ref, v_ref, w_ref, att_ref, far_ref, mid_ref):
    rows, width = q_ref.shape
    half = rows // 2
    for h in range(width // HD):
        cols = slice(h * HD, (h + 1) * HD)
        for c in range(2):
            att_ref[c * half : (c + 1) * half, cols] = attend(
                q_ref[c * half : (c + 1) * half, cols],
                k_ref[: (c + 1) * half, cols],
                v_ref[: (c + 1) * half, cols],
                len_ref,
                c * half,
            )
    att = att_ref[...]
    part = far_ref.shape[1]
    far_ref[...] = dot(att, w_ref[:, pl.ds(pl.multiple_of(col_far() * part, part), part)], (1, 0)).astype(BF16)
    mid_ref[...] = dot(att, w_ref[:, pl.ds(pl.multiple_of(col_mid() * part, part), part)], (1, 0))


def project_kernel(col_near, col_own, att_ref, w_ref, near_ref, own_ref):
    att = att_ref[...]
    part = near_ref.shape[1]
    near_ref[...] = dot(att, w_ref[:, pl.ds(pl.multiple_of(col_near() * part, part), part)], (1, 0)).astype(BF16)
    own_ref[...] = dot(att, w_ref[:, pl.ds(pl.multiple_of(col_own() * part, part), part)], (1, 0))


def place(ids_ref, home_ref, s):
    return home_ref[ids_ref[0, s]] ^ lax.axis_index("req")


def low_kernel(len_ref, ids_ref, home_ref, att_ref, fac_ref, low_ref):
    rank, rows = low_ref.shape
    prompts = len_ref.shape[1]
    downs = jnp.concatenate([fac_ref[place(ids_ref, home_ref, s), :rank, :] for s in range(prompts)], axis=0)
    every = dot(downs, att_ref[...], (1, 1))
    position = lax.broadcasted_iota(jnp.int32, (rank, rows), 1)
    low = jnp.zeros((rank, rows), F32)
    for s in range(prompts):
        low = jnp.where(prompt_mask(len_ref, s, position), every[s * rank : (s + 1) * rank], low)
    low_ref[...] = low


def final_kernel(len_ref, ids_ref, home_ref, own_ref, near_ref, far_ref, l0, l1, l2, l3, fac_ref, out_ref):
    rank, rows = l0.shape
    prompts = len_ref.shape[1]
    low = (l0[...] + l1[...]) + (l2[...] + l3[...])
    position = lax.broadcasted_iota(jnp.int32, (rank, rows), 1)
    spread = jnp.concatenate([jnp.where(prompt_mask(len_ref, s, position), low, 0.0) for s in range(prompts)], axis=0)
    uppers = jnp.concatenate([fac_ref[place(ids_ref, home_ref, s), rank:, :] for s in range(prompts)], axis=0)
    high = spread.astype(BF16)
    rest = (spread - high.astype(F32)).astype(BF16)
    delta = dot(high, uppers, (0, 0)) + dot(rest, uppers, (0, 0))
    base = own_ref[...] + near_ref[...].astype(F32) + far_ref[...].astype(F32)
    out_ref[...] = (base + delta).astype(BF16)


def swap(array, axis, size, k):
    return lax.ppermute(array, axis, [(i, i ^ k) for i in range(size)])


def body(n_req, n_tp, queries, key_rows, value_rows, lengths, adapter_ids, adapter_home, adapter_down, adapter_up, output_weight):
    rows, width = queries.shape
    part = output_weight.shape[1] // n_tp
    rank = adapter_down.shape[2]
    shape = jax.ShapeDtypeStruct
    col = lambda k: lambda: lax.axis_index("tp") ^ k

    own_up = lax.dynamic_slice_in_dim(adapter_up[0], lax.axis_index("tp") * part, part, 1)
    factors = jnp.concatenate([adapter_down[0].T, own_up], axis=0)[None]
    gathered = GATHER(factors, n_req)

    att, far_part, mid_part = pl.pallas_call(
        functools.partial(attend_kernel, col(3), col(2)),
        in_specs=[SMEM] + [VMEM] * 4,
        out_specs=[VMEM] * 3,
        out_shape=[shape((rows, width), BF16), shape((rows, part), BF16), shape((rows, part), F32)],
        name="attend",
    )(lengths, queries, key_rows, value_rows, output_weight)
    from_near = swap(far_part, "tp", n_tp, 1)
    to_far = (mid_part + from_near.astype(F32)).astype(BF16)
    from_far = swap(to_far, "tp", n_tp, 2)
    near_part, own_part = pl.pallas_call(
        functools.partial(project_kernel, col(1), col(0)),
        in_specs=[VMEM] * 2,
        out_specs=[VMEM] * 2,
        out_shape=[shape((rows, part), BF16), shape((rows, part), F32)],
        name="project",
    )(att, output_weight)
    near = swap(near_part, "tp", n_tp, 1)
    low = pl.pallas_call(
        low_kernel,
        in_specs=[SMEM] * 3 + [VMEM] * 2,
        out_specs=VMEM,
        out_shape=shape((rank, rows), F32),
        name="low",
    )(lengths, adapter_ids, adapter_home, att, gathered)
    lows = [low] + [swap(low, "tp", n_tp, k) for k in (1, 2, 3)]
    return pl.pallas_call(
        final_kernel,
        in_specs=[SMEM] * 3 + [VMEM] * 8,
        out_specs=VMEM,
        out_shape=shape((rows, part), BF16),
        name="final",
    )(lengths, adapter_ids, adapter_home, own_part, near, from_far, *lows, gathered)


def GATHER(block, n_req):
    step = 1
    while step < n_req:
        block = jnp.concatenate([block, swap(block, "req", n_req, step)], axis=0)
        step *= 2
    return block


def solution(mesh):
    return jax.shard_map(
        functools.partial(body, mesh.shape["req"], mesh.shape["tp"]),
        mesh=mesh,
        in_specs=(
            P("req", "tp"),
            P("req", "tp"),
            P("req", "tp"),
            P("req", None),
            P("req", None),
            P(),
            P("req", "tp", None),
            P("req", None, None),
            P("tp", None),
        ),
        out_specs=P("req", "tp"),
        check_vma=False,
    )
```

```python
import functools
import math

import jax
import jax.numpy as jnp
from jax import lax
from jax.experimental import pallas as pl
from jax.experimental.pallas import tpu as pltpu
from jax.sharding import PartitionSpec as P

HD = 128
VMEM = pl.BlockSpec(memory_space=pltpu.VMEM)
HBM = pl.BlockSpec(memory_space=pltpu.HBM)
F32, BF16 = jnp.float32, jnp.bfloat16


def dot(a, b, contract):
    return lax.dot_general(a, b, ((contract[0:1], contract[1:2]), ((), ())), preferred_element_type=F32)


def attend_kernel(
    hops,
    q_hbm,
    k_hbm,
    v_hbm,
    w_hbm,
    len_hbm,
    ids_hbm,
    home_hbm,
    att_ref,
    place_ref,
    far_ref,
    near_ref,
    mid_ref,
    own_ref,
    q_ref,
    k_ref,
    v_ref,
    w_ref,
    len_ref,
    ids_ref,
    home_ref,
    sems,
):
    rows, width = q_ref.shape
    pairs = (
        (len_hbm, len_ref),
        (ids_hbm, ids_ref),
        (home_hbm, home_ref),
        (q_hbm, q_ref),
        (k_hbm, k_ref),
        (v_hbm, v_ref),
        (w_hbm, w_ref),
    )
    copies = [pltpu.make_async_copy(source, target, sems.at[i]) for i, (source, target) in enumerate(pairs)]
    for copy in copies:
        copy.start()
    for copy in copies[:3]:
        copy.wait()

    me = lax.axis_index("req")
    row_at = lax.broadcasted_iota(jnp.int32, (rows, 1), 0)
    col_at = lax.broadcasted_iota(jnp.int32, place_ref.shape, 1)
    start, boundary = jnp.zeros((rows, 1), jnp.int32), jnp.int32(0)
    place = jnp.zeros(place_ref.shape, jnp.int32)
    for s in range(len_ref.shape[1]):
        distance = home_ref[ids_ref[0, s]] ^ me
        spot = sum((jnp.where((distance & k) != 0, 1 << j, 0) for j, k in enumerate(hops)), jnp.int32(0))
        start = jnp.where(row_at >= boundary, boundary, start)
        place = jnp.where(col_at >= boundary, spot, place)
        boundary += len_ref[0, s]
    place_ref[...] = place

    half = rows // 2
    items = [(h, c * half, (c + 1) * half) for h in range(width // HD) for c in range(2)]
    allowed = {}
    for _, low, high in items[:2]:
        query_at = low + lax.broadcasted_iota(jnp.int32, (half, 1), 0)
        key_at = lax.broadcasted_iota(jnp.int32, (half, high), 1)
        allowed[low] = (key_at >= start[low:high]) & (key_at <= query_at)
    copies[3].wait()
    copies[4].wait()
    scores = [
        dot(q_ref[low:high, h * HD : (h + 1) * HD], k_ref[:high, h * HD : (h + 1) * HD], (1, 1)) for h, low, high in items
    ]
    weights = []
    for score, (h, low, high) in zip(scores, items):
        masked = jnp.where(allowed[low], score * (1.0 / math.sqrt(HD)), -1e30)
        exponent = jnp.exp(masked - jnp.max(masked, axis=1, keepdims=True))
        weights.append((exponent * (1.0 / jnp.sum(exponent, axis=1, keepdims=True))).astype(BF16))
    copies[5].wait()
    mixed = [
        dot(weight, v_ref[:high, h * HD : (h + 1) * HD], (1, 0)).astype(BF16)
        for weight, (h, low, high) in zip(weights, items)
    ]
    for value, (h, low, high) in zip(mixed, items):
        att_ref[low:high, h * HD : (h + 1) * HD] = value

    att = att_ref[...]
    part = far_ref.shape[1]
    mine = lax.axis_index("tp")
    copies[6].wait()
    for k, ref in ((3, far_ref), (2, mid_ref), (1, near_ref), (0, own_ref)):
        block = w_ref[:, pl.ds(pl.multiple_of((mine ^ k) * part, part), part)]
        ref[...] = dot(att, block, (1, 0)).astype(ref.dtype)


def of_prompt(place_ref, rank, blocks):
    row_place = lax.broadcasted_iota(jnp.int32, (blocks * rank, place_ref.shape[1]), 0) // rank
    return row_place == place_ref[0:1, :]


def low_kernel(place_ref, att_ref, held_ref, came_ref, low_ref):
    rank, rows = low_ref.shape
    blocks, _, width = held_ref.shape
    chosen = of_prompt(place_ref, rank, 2 * blocks)
    total = jnp.zeros((rank, rows), F32)
    for n, ref in enumerate((held_ref, came_ref)):
        every = dot(ref[...].reshape(blocks * rank, width), att_ref[...], (1, 1))
        every = jnp.where(chosen[n * blocks * rank : (n + 1) * blocks * rank], every, 0.0)
        total += jnp.sum(every.reshape(blocks, rank, rows), axis=0)
    low_ref[...] = total


def final_kernel(place_ref, own_ref, near_ref, far_ref, low0_ref, low1_ref, held_ref, came_ref, out_ref):
    rank, rows = low0_ref.shape
    blocks, _, part = held_ref.shape
    low = low0_ref[...] + low1_ref[...]
    spread = jnp.where(of_prompt(place_ref, rank, 2 * blocks), jnp.concatenate([low] * (2 * blocks), axis=0), 0.0)
    uppers = jnp.concatenate([ref[...].reshape(blocks * rank, part) for ref in (held_ref, came_ref)], axis=0)
    high = spread.astype(BF16)
    rest = (spread - high.astype(F32)).astype(BF16)
    delta = dot(high, uppers, (0, 0)) + dot(rest, uppers, (0, 0))
    base = own_ref[...] + near_ref[...].astype(F32) + far_ref[...].astype(F32)
    out_ref[...] = (base + delta).astype(BF16)


def swap(array, axis, size, k):
    return lax.ppermute(array, axis, [(i, i ^ k) for i in range(size)])


def call(kernel, name, operands, specs, out, mib, us, scratch=(), place=pltpu.VMEM):
    return pl.pallas_call(
        kernel,
        in_specs=specs,
        out_specs=[VMEM] * len(out),
        out_shape=[place(s, d) for s, d in out],
        scratch_shapes=scratch,
        compiler_params=pltpu.CompilerParams(vmem_limit_bytes=mib << 20),
        cost_estimate=pl.CostEstimate(flops=int(us * 1e9), bytes_accessed=int(us * 3.6e6), transcendentals=0),
        name=name,
    )(*operands)


def body(n_req, n_tp, queries, key_rows, value_rows, lengths, adapter_ids, adapter_home, adapter_down, adapter_up, output_weight):
    rows, width = queries.shape
    part = output_weight.shape[1] // n_tp
    rank = adapter_down.shape[2]
    hops = [n_req >> (j + 1) for j in range(n_req.bit_length() - 1)]
    tie = lax.optimization_barrier

    own_up = lax.dynamic_slice_in_dim(adapter_up[0], lax.axis_index("tp") * part, part, 1)
    held = jnp.concatenate([adapter_down[0].T, own_up], axis=0)[None]
    queries, held = tie((queries, held))
    inputs = [
        pltpu.with_memory_space_constraint(a, pltpu.HBM)
        for a in (queries, key_rows, value_rows, output_weight, lengths, adapter_ids, adapter_home)
    ]
    att, place, far_part, near_part, mid_part, own_part = call(
        functools.partial(attend_kernel, hops),
        "attend",
        inputs,
        [HBM] * 7,
        [((rows, width), BF16), ((8, rows), jnp.int32)] + [((rows, part), BF16)] * 2 + [((rows, part), F32)] * 2,
        16,
        3,
        [pltpu.VMEM(a.shape, a.dtype) for a in inputs[:4]]
        + [pltpu.SMEM(a.shape, a.dtype) for a in inputs[4:]]
        + [pltpu.SemaphoreType.DMA((7,))],
    )
    came = swap(held, "req", n_req, hops[0])
    held, came, far_part, near_part = tie((held, came, far_part, near_part))
    held = jnp.concatenate([held, came], axis=0)
    from_near = swap(far_part, "tp", n_tp, 1)
    near = swap(near_part, "tp", n_tp, 1)
    to_far = (mid_part + from_near.astype(F32)).astype(BF16)
    from_far = swap(to_far, "tp", n_tp, 2)
    for j, k in enumerate(hops[1:-1]):
        came = swap(held, "req", n_req, k)
        if j == 0:
            held, came, _ = tie((held, came, to_far))
        held = jnp.concatenate([held, came], axis=0)
    downs, ups = held[:, :rank], held[:, rank:]
    downs_came = swap(downs, "req", n_req, hops[-1])
    ups_came = swap(ups, "req", n_req, hops[-1])

    (low,) = call(low_kernel, "low", (place, att, downs, downs_came), [VMEM] * 4, [((rank, rows), F32)], 16, 0.3)
    low = low + swap(low, "tp", n_tp, 1)
    (out,) = call(
        final_kernel,
        "final",
        (place, own_part, near, from_far, low, swap(low, "tp", n_tp, 2), ups, ups_came),
        [VMEM] * 8,
        [((rows, part), BF16)],
        24,
        1,
        place=jax.ShapeDtypeStruct,
    )
    return out


def solution(mesh):
    return jax.shard_map(
        functools.partial(body, mesh.shape["req"], mesh.shape["tp"]),
        mesh=mesh,
        in_specs=(
            P("req", "tp"),
            P("req", "tp"),
            P("req", "tp"),
            P("req", None),
            P("req", None),
            P(),
            P("req", "tp", None),
            P("req", None, None),
            P("tp", None),
        ),
        out_specs=P("req", "tp"),
        check_vma=False,
    )
```

```python
import functools
import math

import jax
import jax.numpy as jnp
from jax import lax
from jax.experimental import pallas as pl
from jax.experimental.pallas import tpu as pltpu
from jax.sharding import PartitionSpec as P

HD = 128
VMEM = pl.BlockSpec(memory_space=pltpu.VMEM)
HBM = pl.BlockSpec(memory_space=pltpu.HBM)
F32, BF16 = jnp.float32, jnp.bfloat16


def dot(a, b, contract):
    return lax.dot_general(a, b, ((contract[0:1], contract[1:2]), ((), ())), preferred_element_type=F32)


def attend_kernel(
    hops,
    q_hbm,
    k_hbm,
    v_hbm,
    w_hbm,
    len_hbm,
    ids_hbm,
    home_hbm,
    att_ref,
    place_ref,
    far_ref,
    near_ref,
    mid_ref,
    own_ref,
    q_ref,
    k_ref,
    v_ref,
    w_ref,
    len_ref,
    ids_ref,
    home_ref,
    sems,
):
    rows, width = q_ref.shape
    pairs = (
        (len_hbm, len_ref),
        (ids_hbm, ids_ref),
        (home_hbm, home_ref),
        (q_hbm, q_ref),
        (k_hbm, k_ref),
        (v_hbm, v_ref),
        (w_hbm, w_ref),
    )
    copies = [pltpu.make_async_copy(source, target, sems.at[i]) for i, (source, target) in enumerate(pairs)]
    for copy in copies:
        copy.start()
    for copy in copies[:3]:
        copy.wait()

    me = lax.axis_index("req")
    row_at = lax.broadcasted_iota(jnp.int32, (rows, 1), 0)
    col_at = lax.broadcasted_iota(jnp.int32, place_ref.shape, 1)
    start, boundary = jnp.zeros((rows, 1), jnp.int32), jnp.int32(0)
    place = jnp.zeros(place_ref.shape, jnp.int32)
    for s in range(len_ref.shape[1]):
        distance = home_ref[ids_ref[0, s]] ^ me
        spot = sum((jnp.where((distance & k) != 0, 1 << j, 0) for j, k in enumerate(hops)), jnp.int32(0))
        start = jnp.where(row_at >= boundary, boundary, start)
        place = jnp.where(col_at >= boundary, spot, place)
        boundary += len_ref[0, s]
    place_ref[...] = place

    half = rows // 2
    items = [(h, c * half, (c + 1) * half) for h in range(width // HD) for c in range(2)]
    allowed = {}
    for _, low, high in items[:2]:
        query_at = low + lax.broadcasted_iota(jnp.int32, (half, 1), 0)
        key_at = lax.broadcasted_iota(jnp.int32, (half, high), 1)
        allowed[low] = (key_at >= start[low:high]) & (key_at <= query_at)
    copies[3].wait()
    copies[4].wait()
    scores = [
        dot(q_ref[low:high, h * HD : (h + 1) * HD], k_ref[:high, h * HD : (h + 1) * HD], (1, 1)) for h, low, high in items
    ]
    weights = []
    for score, (h, low, high) in zip(scores, items):
        masked = jnp.where(allowed[low], score * (1.0 / math.sqrt(HD)), -1e30)
        exponent = jnp.exp(masked - jnp.max(masked, axis=1, keepdims=True))
        weights.append((exponent * (1.0 / jnp.sum(exponent, axis=1, keepdims=True))).astype(BF16))
    copies[5].wait()
    mixed = [
        dot(weight, v_ref[:high, h * HD : (h + 1) * HD], (1, 0)).astype(BF16)
        for weight, (h, low, high) in zip(weights, items)
    ]
    for value, (h, low, high) in zip(mixed, items):
        att_ref[low:high, h * HD : (h + 1) * HD] = value

    att = att_ref[...]
    part = far_ref.shape[1]
    mine = lax.axis_index("tp")
    copies[6].wait()
    for k, ref in ((3, far_ref), (2, mid_ref), (1, near_ref), (0, own_ref)):
        block = w_ref[:, pl.ds(pl.multiple_of((mine ^ k) * part, part), part)]
        ref[...] = dot(att, block, (1, 0)).astype(ref.dtype)


def of_prompt(place_ref, rank, blocks):
    row_place = lax.broadcasted_iota(jnp.int32, (blocks * rank, place_ref.shape[1]), 0) // rank
    return row_place == place_ref[0:1, :]


def low_kernel(place_ref, att_ref, held_ref, came_ref, low_ref):
    rank, rows = low_ref.shape
    blocks, _, width = held_ref.shape
    chosen = of_prompt(place_ref, rank, 2 * blocks)
    total = jnp.zeros((rank, rows), F32)
    for n, ref in enumerate((held_ref, came_ref)):
        every = dot(ref[...].reshape(blocks * rank, width), att_ref[...], (1, 1))
        every = jnp.where(chosen[n * blocks * rank : (n + 1) * blocks * rank], every, 0.0)
        total += jnp.sum(every.reshape(blocks, rank, rows), axis=0)
    low_ref[...] = total


def final_kernel(place_ref, own_ref, near_ref, far_ref, low0_ref, low1_ref, held_ref, came_ref, out_ref):
    rank, rows = low0_ref.shape
    blocks, _, part = held_ref.shape
    low = low0_ref[...] + low1_ref[...]
    spread = jnp.where(of_prompt(place_ref, rank, 2 * blocks), jnp.concatenate([low] * (2 * blocks), axis=0), 0.0)
    uppers = jnp.concatenate([ref[...].reshape(blocks * rank, part) for ref in (held_ref, came_ref)], axis=0)
    high = spread.astype(BF16)
    rest = (spread - high.astype(F32)).astype(BF16)
    delta = dot(high, uppers, (0, 0)) + dot(rest, uppers, (0, 0))
    base = own_ref[...] + near_ref[...].astype(F32) + far_ref[...].astype(F32)
    out_ref[...] = (base + delta).astype(BF16)


def swap(array, axis, size, k):
    return lax.ppermute(array, axis, [(i, i ^ k) for i in range(size)])


def call(kernel, name, operands, specs, out, mib, us, scratch=(), place=pltpu.VMEM):
    return pl.pallas_call(
        kernel,
        in_specs=specs,
        out_specs=[VMEM] * len(out),
        out_shape=[place(s, d) for s, d in out],
        scratch_shapes=scratch,
        compiler_params=pltpu.CompilerParams(vmem_limit_bytes=mib << 20),
        cost_estimate=pl.CostEstimate(flops=int(us * 1e9), bytes_accessed=int(us * 3.6e6), transcendentals=0),
        name=name,
    )(*operands)


def body(n_req, n_tp, queries, key_rows, value_rows, lengths, adapter_ids, adapter_home, adapter_down, adapter_up, output_weight):
    rows, width = queries.shape
    part = output_weight.shape[1] // n_tp
    rank = adapter_down.shape[2]
    hops = [n_req >> (j + 1) for j in range(n_req.bit_length() - 1)]
    tie = lax.optimization_barrier

    own_up = lax.dynamic_slice_in_dim(adapter_up[0], lax.axis_index("tp") * part, part, 1)
    held = jnp.concatenate([adapter_down[0].T, own_up], axis=0)[None]
    queries, held = tie((queries, held))
    inputs = [
        pltpu.with_memory_space_constraint(a, pltpu.HBM)
        for a in (queries, key_rows, value_rows, output_weight, lengths, adapter_ids, adapter_home)
    ]
    att, place, far_part, near_part, mid_part, own_part = call(
        functools.partial(attend_kernel, hops),
        "attend",
        inputs,
        [HBM] * 7,
        [((rows, width), BF16), ((8, rows), jnp.int32)] + [((rows, part), BF16)] * 2 + [((rows, part), F32)] * 2,
        16,
        3,
        [pltpu.VMEM(a.shape, a.dtype) for a in inputs[:4]]
        + [pltpu.SMEM(a.shape, a.dtype) for a in inputs[4:]]
        + [pltpu.SemaphoreType.DMA((7,))],
    )
    came = swap(held, "req", n_req, hops[0])
    held, came, far_part, near_part = tie((held, came, far_part, near_part))
    held = jnp.concatenate([held, came], axis=0)
    from_near = swap(far_part, "tp", n_tp, 1)
    near = swap(near_part, "tp", n_tp, 1)
    to_far = (mid_part + from_near.astype(F32)).astype(BF16)
    from_far = swap(to_far, "tp", n_tp, 2)
    for j, k in enumerate(hops[1:-1]):
        came = swap(held, "req", n_req, k)
        if j == 0:
            held, came, _ = tie((held, came, to_far))
        held = jnp.concatenate([held, came], axis=0)
    downs, ups = held[:, :rank], held[:, rank:]
    downs_came = swap(downs, "req", n_req, hops[-1])
    ups_came = swap(ups, "req", n_req, hops[-1])

    (low,) = call(low_kernel, "low", (place, att, downs, downs_came), [VMEM] * 4, [((rank, rows), F32)], 16, 0.3)
    low = low + swap(low, "tp", n_tp, 1)
    (out,) = call(
        final_kernel,
        "final",
        (place, own_part, near, from_far, low, swap(low, "tp", n_tp, 3), ups, ups_came),
        [VMEM] * 8,
        [((rows, part), BF16)],
        24,
        1,
        place=jax.ShapeDtypeStruct,
    )
    return out


def solution(mesh):
    return jax.shard_map(
        functools.partial(body, mesh.shape["req"], mesh.shape["tp"]),
        mesh=mesh,
        in_specs=(
            P("req", "tp"),
            P("req", "tp"),
            P("req", "tp"),
            P("req", None),
            P("req", None),
            P(),
            P("req", "tp", None),
            P("req", None, None),
            P("tp", None),
        ),
        out_specs=P("req", "tp"),
        check_vma=False,
    )
```

```python
import functools
import math

import jax
import jax.numpy as jnp
from jax import lax
from jax.experimental import pallas as pl
from jax.experimental.pallas import tpu as pltpu
from jax.sharding import PartitionSpec as P

HD = 128
VMEM = pl.BlockSpec(memory_space=pltpu.VMEM)
HBM = pl.BlockSpec(memory_space=pltpu.HBM)
F32, BF16 = jnp.float32, jnp.bfloat16
CHUNKS = 2


def dot(a, b, contract):
    return lax.dot_general(a, b, ((contract[0:1], contract[1:2]), ((), ())), preferred_element_type=F32)


def attend_kernel(
    hops,
    q_hbm,
    k_hbm,
    v_hbm,
    w_hbm,
    len_hbm,
    ids_hbm,
    home_hbm,
    att_ref,
    place_ref,
    far_ref,
    near_ref,
    mid_ref,
    own_ref,
    q_ref,
    k_ref,
    v_ref,
    w_ref,
    len_ref,
    ids_ref,
    home_ref,
    sems,
):
    rows, width = q_ref.shape
    pairs = (
        (len_hbm, len_ref),
        (ids_hbm, ids_ref),
        (home_hbm, home_ref),
        (q_hbm, q_ref),
        (k_hbm, k_ref),
        (v_hbm, v_ref),
        (w_hbm, w_ref),
    )
    copies = [pltpu.make_async_copy(source, target, sems.at[i]) for i, (source, target) in enumerate(pairs)]
    for copy in copies:
        copy.start()
    for copy in copies[:3]:
        copy.wait()

    me = lax.axis_index("req")
    row_at = lax.broadcasted_iota(jnp.int32, (rows, 1), 0)
    col_at = lax.broadcasted_iota(jnp.int32, place_ref.shape, 1)
    start, boundary = jnp.zeros((rows, 1), jnp.int32), jnp.int32(0)
    place = jnp.zeros(place_ref.shape, jnp.int32)
    for s in range(len_ref.shape[1]):
        distance = home_ref[ids_ref[0, s]] ^ me
        spot = sum((jnp.where((distance & k) != 0, 1 << j, 0) for j, k in enumerate(hops)), jnp.int32(0))
        start = jnp.where(row_at >= boundary, boundary, start)
        place = jnp.where(col_at >= boundary, spot, place)
        boundary += len_ref[0, s]
    place_ref[...] = place

    half = rows // 2
    items = [(h, c * half, (c + 1) * half) for h in range(width // HD) for c in range(2)]
    allowed = {}
    for _, low, high in items[:2]:
        query_at = low + lax.broadcasted_iota(jnp.int32, (half, 1), 0)
        key_at = lax.broadcasted_iota(jnp.int32, (half, high), 1)
        allowed[low] = (key_at >= start[low:high]) & (key_at <= query_at)
    copies[3].wait()
    copies[4].wait()
    scores = [
        dot(q_ref[low:high, h * HD : (h + 1) * HD], k_ref[:high, h * HD : (h + 1) * HD], (1, 1)) for h, low, high in items
    ]
    weights = []
    for score, (h, low, high) in zip(scores, items):
        masked = jnp.where(allowed[low], score * (1.0 / math.sqrt(HD)), -1e30)
        exponent = jnp.exp(masked - jnp.max(masked, axis=1, keepdims=True))
        weights.append((exponent * (1.0 / jnp.sum(exponent, axis=1, keepdims=True))).astype(BF16))
    copies[5].wait()
    mixed = [
        dot(weight, v_ref[:high, h * HD : (h + 1) * HD], (1, 0)).astype(BF16)
        for weight, (h, low, high) in zip(weights, items)
    ]
    for value, (h, low, high) in zip(mixed, items):
        att_ref[low:high, h * HD : (h + 1) * HD] = value

    att = att_ref[...]
    part = far_ref.shape[1]
    mine = lax.axis_index("tp")
    copies[6].wait()
    for k, ref in ((2, far_ref), (3, mid_ref), (1, near_ref), (0, own_ref)):
        block = w_ref[:, pl.ds(pl.multiple_of((mine ^ k) * part, part), part)]
        ref[...] = dot(att, block, (1, 0)).astype(ref.dtype)


def of_prompt(place_ref, rank, blocks):
    row_place = lax.broadcasted_iota(jnp.int32, (blocks * rank, place_ref.shape[1]), 0) // rank
    return row_place == place_ref[0:1, :]


def low_kernel(place_ref, att_ref, held_ref, came_ref, low_ref):
    rank, rows = low_ref.shape
    blocks, _, width = held_ref.shape
    chosen = of_prompt(place_ref, rank, 2 * blocks)
    total = jnp.zeros((rank, rows), F32)
    for n, ref in enumerate((held_ref, came_ref)):
        every = dot(ref[...].reshape(blocks * rank, width), att_ref[...], (1, 1))
        every = jnp.where(chosen[n * blocks * rank : (n + 1) * blocks * rank], every, 0.0)
        total += jnp.sum(every.reshape(blocks, rank, rows), axis=0)
    low_ref[...] = total


def base_kernel(own_ref, near_ref, far_ref, base_ref):
    base_ref[...] = own_ref[...] + near_ref[...].astype(F32) + far_ref[...].astype(F32)


def final_kernel(place_ref, base_ref, low0_ref, low1_ref, low2_ref, low3_ref, held_ref, came_ref, out_hbm, out_ref, sems):
    rank, rows = low0_ref.shape
    blocks, _, part = held_ref.shape
    low = (low0_ref[...] + low1_ref[...]) + (low2_ref[...] + low3_ref[...])
    spread = jnp.where(of_prompt(place_ref, rank, 2 * blocks), jnp.concatenate([low] * (2 * blocks), axis=0), 0.0)
    uppers = jnp.concatenate([ref[...].reshape(blocks * rank, part) for ref in (held_ref, came_ref)], axis=0)
    high = spread.astype(BF16)
    rest = (spread - high.astype(F32)).astype(BF16)
    copies = []
    for c in range(CHUNKS):
        mine = slice(c * rows // CHUNKS, (c + 1) * rows // CHUNKS)
        delta = dot(high[:, mine], uppers, (0, 0)) + dot(rest[:, mine], uppers, (0, 0))
        out_ref[mine, :] = (base_ref[mine, :] + delta).astype(BF16)
        copies.append(pltpu.make_async_copy(out_ref.at[mine], out_hbm.at[mine], sems.at[c]))
        copies[-1].start()
    for copy in copies:
        copy.wait()


def swap(array, axis, size, k):
    return lax.ppermute(array, axis, [(i, i ^ k) for i in range(size)])


def call(kernel, name, operands, specs, out, mib, us, scratch=(), place=pltpu.VMEM, out_spec=VMEM):
    return pl.pallas_call(
        kernel,
        in_specs=specs,
        out_specs=[out_spec] * len(out),
        out_shape=[place(s, d) for s, d in out],
        scratch_shapes=scratch,
        compiler_params=pltpu.CompilerParams(vmem_limit_bytes=mib << 20),
        cost_estimate=pl.CostEstimate(flops=int(us * 1e9), bytes_accessed=int(us * 3.6e6), transcendentals=0),
        name=name,
    )(*operands)


def body(n_req, n_tp, queries, key_rows, value_rows, lengths, adapter_ids, adapter_home, adapter_down, adapter_up, output_weight):
    rows, width = queries.shape
    part = output_weight.shape[1] // n_tp
    rank = adapter_down.shape[2]
    hops = [n_req >> (j + 1) for j in range(n_req.bit_length() - 1)]
    tie = lax.optimization_barrier

    own_up = lax.dynamic_slice_in_dim(adapter_up[0], lax.axis_index("tp") * part, part, 1)
    held = jnp.concatenate([adapter_down[0].T, own_up], axis=0)[None]
    queries, held = tie((queries, held))
    inputs = [
        pltpu.with_memory_space_constraint(a, pltpu.HBM)
        for a in (queries, key_rows, value_rows, output_weight, lengths, adapter_ids, adapter_home)
    ]
    att, place, far_part, near_part, mid_part, own_part = call(
        functools.partial(attend_kernel, hops),
        "attend",
        inputs,
        [HBM] * 7,
        [((rows, width), BF16), ((8, rows), jnp.int32)] + [((rows, part), BF16)] * 2 + [((rows, part), F32)] * 2,
        16,
        3,
        [pltpu.VMEM(a.shape, a.dtype) for a in inputs[:4]]
        + [pltpu.SMEM(a.shape, a.dtype) for a in inputs[4:]]
        + [pltpu.SemaphoreType.DMA((7,))],
    )
    came = swap(held, "req", n_req, hops[0])
    held, came, far_part, near_part = tie((held, came, far_part, near_part))
    held = jnp.concatenate([held, came], axis=0)
    from_near = swap(far_part, "tp", n_tp, 1)
    near = swap(near_part, "tp", n_tp, 1)
    to_far = (mid_part + from_near.astype(F32)).astype(BF16)
    from_far = swap(to_far, "tp", n_tp, 3)
    for j, k in enumerate(hops[1:-1]):
        came = swap(held, "req", n_req, k)
        if j == 0:
            held, came, _ = tie((held, came, to_far))
        held = jnp.concatenate([held, came], axis=0)
    downs, ups = held[:, :rank], held[:, rank:]
    downs_came = swap(downs, "req", n_req, hops[-1])
    ups_came = swap(ups, "req", n_req, hops[-1])

    (low,) = call(low_kernel, "low", (place, att, downs, downs_came), [VMEM] * 4, [((rank, rows), F32)], 16, 0.3)
    lows = [low] + [swap(low, "tp", n_tp, k) for k in (3, 2, 1)]
    (base,) = call(base_kernel, "base", (own_part, near, from_far), [VMEM] * 3, [((rows, part), F32)], 8, 0.2)
    (out,) = call(
        final_kernel,
        "final",
        (place, base, *lows, ups, ups_came),
        [VMEM] * 8,
        [((rows, part), BF16)],
        24,
        1,
        [pltpu.VMEM((rows, part), BF16), pltpu.SemaphoreType.DMA((CHUNKS,))],
        jax.ShapeDtypeStruct,
        HBM,
    )
    return out


def solution(mesh):
    return jax.shard_map(
        functools.partial(body, mesh.shape["req"], mesh.shape["tp"]),
        mesh=mesh,
        in_specs=(
            P("req", "tp"),
            P("req", "tp"),
            P("req", "tp"),
            P("req", None),
            P("req", None),
            P(),
            P("req", "tp", None),
            P("req", None, None),
            P("tp", None),
        ),
        out_specs=P("req", "tp"),
        check_vma=False,
    )
```

```python
import functools
import math

import jax
import jax.numpy as jnp
from jax import lax
from jax.experimental import pallas as pl
from jax.experimental.pallas import tpu as pltpu
from jax.sharding import PartitionSpec as P

HD = 128
VMEM = pl.BlockSpec(memory_space=pltpu.VMEM)
HBM = pl.BlockSpec(memory_space=pltpu.HBM)
F32, BF16 = jnp.float32, jnp.bfloat16
CHUNKS = 2


def dot(a, b, contract):
    return lax.dot_general(a, b, ((contract[0:1], contract[1:2]), ((), ())), preferred_element_type=F32)


def attend_kernel(
    hops,
    q_hbm,
    k_hbm,
    v_hbm,
    w_hbm,
    len_hbm,
    ids_hbm,
    home_hbm,
    att_ref,
    place_ref,
    far_ref,
    near_ref,
    mid_ref,
    own_ref,
    q_ref,
    k_ref,
    v_ref,
    w_ref,
    len_ref,
    ids_ref,
    home_ref,
    sems,
):
    rows, width = q_ref.shape
    pairs = (
        (len_hbm, len_ref),
        (ids_hbm, ids_ref),
        (home_hbm, home_ref),
        (q_hbm, q_ref),
        (k_hbm, k_ref),
        (v_hbm, v_ref),
        (w_hbm, w_ref),
    )
    copies = [pltpu.make_async_copy(source, target, sems.at[i]) for i, (source, target) in enumerate(pairs)]
    for copy in copies:
        copy.start()
    for copy in copies[:3]:
        copy.wait()

    me = lax.axis_index("req")
    row_at = lax.broadcasted_iota(jnp.int32, (rows, 1), 0)
    col_at = lax.broadcasted_iota(jnp.int32, place_ref.shape, 1)
    start, boundary = jnp.zeros((rows, 1), jnp.int32), jnp.int32(0)
    place = jnp.zeros(place_ref.shape, jnp.int32)
    for s in range(len_ref.shape[1]):
        distance = home_ref[ids_ref[0, s]] ^ me
        spot = sum((jnp.where((distance & k) != 0, 1 << j, 0) for j, k in enumerate(hops)), jnp.int32(0))
        start = jnp.where(row_at >= boundary, boundary, start)
        place = jnp.where(col_at >= boundary, spot, place)
        boundary += len_ref[0, s]
    place_ref[...] = place

    half = rows // 2
    items = [(h, c * half, (c + 1) * half) for h in range(width // HD) for c in range(2)]
    allowed = {}
    for _, low, high in items[:2]:
        query_at = low + lax.broadcasted_iota(jnp.int32, (half, 1), 0)
        key_at = lax.broadcasted_iota(jnp.int32, (half, high), 1)
        allowed[low] = (key_at >= start[low:high]) & (key_at <= query_at)
    copies[3].wait()
    copies[4].wait()
    scores = [
        dot(q_ref[low:high, h * HD : (h + 1) * HD], k_ref[:high, h * HD : (h + 1) * HD], (1, 1)) for h, low, high in items
    ]
    weights = []
    for score, (h, low, high) in zip(scores, items):
        masked = jnp.where(allowed[low], score * (1.0 / math.sqrt(HD)), -1e30)
        exponent = jnp.exp(masked - jnp.max(masked, axis=1, keepdims=True))
        weights.append((exponent * (1.0 / jnp.sum(exponent, axis=1, keepdims=True))).astype(BF16))
    copies[5].wait()
    mixed = [
        dot(weight, v_ref[:high, h * HD : (h + 1) * HD], (1, 0)).astype(BF16)
        for weight, (h, low, high) in zip(weights, items)
    ]
    for value, (h, low, high) in zip(mixed, items):
        att_ref[low:high, h * HD : (h + 1) * HD] = value

    att = att_ref[...]
    part = far_ref.shape[1]
    mine = lax.axis_index("tp")
    copies[6].wait()
    for k, ref in ((2, far_ref), (3, mid_ref), (1, near_ref), (0, own_ref)):
        block = w_ref[:, pl.ds(pl.multiple_of((mine ^ k) * part, part), part)]
        ref[...] = dot(att, block, (1, 0)).astype(ref.dtype)


def of_prompt(place_ref, rank, blocks):
    row_place = lax.broadcasted_iota(jnp.int32, (blocks * rank, place_ref.shape[1]), 0) // rank
    return row_place == place_ref[0:1, :]


def low_kernel(place_ref, att_ref, held_ref, came_ref, low_ref):
    rank, rows = low_ref.shape
    blocks, _, width = held_ref.shape
    chosen = of_prompt(place_ref, rank, 2 * blocks)
    total = jnp.zeros((rank, rows), F32)
    for n, ref in enumerate((held_ref, came_ref)):
        every = dot(ref[...].reshape(blocks * rank, width), att_ref[...], (1, 1))
        every = jnp.where(chosen[n * blocks * rank : (n + 1) * blocks * rank], every, 0.0)
        total += jnp.sum(every.reshape(blocks, rank, rows), axis=0)
    low_ref[...] = total


def base_kernel(own_ref, near_ref, far_ref, base_ref):
    base_ref[...] = own_ref[...] + near_ref[...].astype(F32) + far_ref[...].astype(F32)


def final_kernel(place_ref, base_ref, low0_ref, low1_ref, low2_ref, low3_ref, held_ref, came_ref, out_hbm, out_ref, sems):
    rank, rows = low0_ref.shape
    blocks, _, part = held_ref.shape
    low = (low0_ref[...] + low1_ref[...]) + (low2_ref[...] + low3_ref[...])
    spread = jnp.where(of_prompt(place_ref, rank, 2 * blocks), jnp.concatenate([low] * (2 * blocks), axis=0), 0.0)
    uppers = jnp.concatenate([ref[...].reshape(blocks * rank, part) for ref in (held_ref, came_ref)], axis=0)
    high = spread.astype(BF16)
    rest = (spread - high.astype(F32)).astype(BF16)
    spread = jnp.concatenate([high, rest], axis=0).T
    uppers = jnp.concatenate([uppers, uppers], axis=0)
    copies = []
    for c in range(CHUNKS):
        mine = slice(c * rows // CHUNKS, (c + 1) * rows // CHUNKS)
        delta = dot(spread[mine], uppers, (1, 0))
        out_ref[mine, :] = (base_ref[mine, :] + delta).astype(BF16)
        copies.append(pltpu.make_async_copy(out_ref.at[mine], out_hbm.at[mine], sems.at[c]))
        copies[-1].start()
    for copy in copies:
        copy.wait()


def swap(array, axis, size, k):
    return lax.ppermute(array, axis, [(i, i ^ k) for i in range(size)])


def call(kernel, name, operands, specs, out, mib, us, scratch=(), place=pltpu.VMEM, out_spec=VMEM):
    return pl.pallas_call(
        kernel,
        in_specs=specs,
        out_specs=[out_spec] * len(out),
        out_shape=[place(s, d) for s, d in out],
        scratch_shapes=scratch,
        compiler_params=pltpu.CompilerParams(vmem_limit_bytes=mib << 20),
        cost_estimate=pl.CostEstimate(flops=int(us * 1e9), bytes_accessed=int(us * 3.6e6), transcendentals=0),
        name=name,
    )(*operands)


def body(n_req, n_tp, queries, key_rows, value_rows, lengths, adapter_ids, adapter_home, adapter_down, adapter_up, output_weight):
    rows, width = queries.shape
    part = output_weight.shape[1] // n_tp
    rank = adapter_down.shape[2]
    hops = [n_req >> (j + 1) for j in range(n_req.bit_length() - 1)]
    tie = lax.optimization_barrier

    own_up = lax.dynamic_slice_in_dim(adapter_up[0], lax.axis_index("tp") * part, part, 1)
    held = jnp.concatenate([adapter_down[0].T, own_up], axis=0)[None]
    queries, held = tie((queries, held))
    inputs = [
        pltpu.with_memory_space_constraint(a, pltpu.HBM)
        for a in (queries, key_rows, value_rows, output_weight, lengths, adapter_ids, adapter_home)
    ]
    att, place, far_part, near_part, mid_part, own_part = call(
        functools.partial(attend_kernel, hops),
        "attend",
        inputs,
        [HBM] * 7,
        [((rows, width), BF16), ((8, rows), jnp.int32)] + [((rows, part), BF16)] * 2 + [((rows, part), F32)] * 2,
        16,
        3,
        [pltpu.VMEM(a.shape, a.dtype) for a in inputs[:4]]
        + [pltpu.SMEM(a.shape, a.dtype) for a in inputs[4:]]
        + [pltpu.SemaphoreType.DMA((7,))],
    )
    came = swap(held, "req", n_req, hops[0])
    held, came, far_part, near_part = tie((held, came, far_part, near_part))
    held = jnp.concatenate([held, came], axis=0)
    from_near = swap(far_part, "tp", n_tp, 1)
    near = swap(near_part, "tp", n_tp, 1)
    to_far = (mid_part + from_near.astype(F32)).astype(BF16)
    from_far = swap(to_far, "tp", n_tp, 3)
    for j, k in enumerate(hops[1:-1]):
        came = swap(held, "req", n_req, k)
        if j == 0:
            held, came, _ = tie((held, came, to_far))
        held = jnp.concatenate([held, came], axis=0)
    downs, ups = held[:, :rank], held[:, rank:]
    downs_came = swap(downs, "req", n_req, hops[-1])
    ups_came = swap(ups, "req", n_req, hops[-1])

    (low,) = call(low_kernel, "low", (place, att, downs, downs_came), [VMEM] * 4, [((rank, rows), F32)], 16, 0.3)
    lows = [low] + [swap(low, "tp", n_tp, k) for k in (3, 2, 1)]
    (base,) = call(base_kernel, "base", (own_part, near, from_far), [VMEM] * 3, [((rows, part), F32)], 8, 0.2)
    (out,) = call(
        final_kernel,
        "final",
        (place, base, *lows, ups, ups_came),
        [VMEM] * 8,
        [((rows, part), BF16)],
        24,
        1,
        [pltpu.VMEM((rows, part), BF16), pltpu.SemaphoreType.DMA((CHUNKS,))],
        jax.ShapeDtypeStruct,
        HBM,
    )
    return out


def solution(mesh):
    return jax.shard_map(
        functools.partial(body, mesh.shape["req"], mesh.shape["tp"]),
        mesh=mesh,
        in_specs=(
            P("req", "tp"),
            P("req", "tp"),
            P("req", "tp"),
            P("req", None),
            P("req", None),
            P(),
            P("req", "tp", None),
            P("req", None, None),
            P("tp", None),
        ),
        out_specs=P("req", "tp"),
        check_vma=False,
    )
```
